32 devices in a mesh: groups: 2 (over x), inst: 8 (over z, y), tp: 2 (over core).
Axes of the slice: x: 2, y: 2, z: 4, core: 2. Of those that a mesh axis runs over, the one named last changes fastest.
Arguments:
- queries: bfloat16 [512, 2, 4096], P(('groups', 'inst'), None, 'tp'), parts along dimension 0, may hold values from -21 to 21
- fresh_keys: bfloat16 [512, 2, 512], P(('groups', 'inst'), None, 'tp'), parts along dimension 0, may hold values from -4 to 4
- fresh_values: bfloat16 [512, 2, 512], P(('groups', 'inst'), None, 'tp'), parts along dimension 0, may hold values from -4 to 4
- cache_keys: bfloat16 [512, 128, 512], P(('groups', 'inst'), None, 'tp'), parts along dimension 0, may hold values from -4 to 4
- cache_values: bfloat16 [512, 128, 512], P(('groups', 'inst'), None, 'tp'), parts along dimension 0, may hold values from -12 to 12
- lengths: int32 [512], P(('groups', 'inst')), parts along dimension 0, may hold values from 1 to 126
- move_rows: int32 [16, 4], P(('groups', 'inst')), parts along dimension 0, may hold values from 0 to 31, as said below
- move_targets: int32 [16, 4], P(('groups', 'inst')), parts along dimension 0, may hold values from 0 to 7, as said below
- move_landing: int32 [16, 4], P(('groups', 'inst')), parts along dimension 0, may hold values from 0 to 31, as said below
Outputs:
- first_mixed: bfloat16 [512, 4096], P(('groups', 'inst'), 'tp'), parts along dimension 0
- second_mixed: bfloat16 [512, 4096], P(('groups', 'inst'), 'tp'), parts along dimension 0
- next_keys: bfloat16 [512, 128, 512], P(('groups', 'inst'), None, 'tp'), parts along dimension 0
- next_values: bfloat16 [512, 128, 512], P(('groups', 'inst'), None, 'tp'), parts along dimension 0
The draws below stay inside these ranges and needn't reach their ends.
There are 2 independent parts, one for each index of `groups`. The reference program is written for one: setup_inputs(seed, part) draws one part's arguments, and reference() takes and returns one part's arrays. A program takes and returns all parts, laid end to end along the dimension named above; each array names one. Nothing has to cross between parts.
Inputs may be any that keep to these rules, and one draw needn't show every extreme that they name: `move_rows`: each instance lists 4 different rows of its own. `move_targets`: never the sending instance; for every list position j the j-th entries of all instances name different instances, so every instance receives exactly 4 rows and at most one from each sender. `move_landing`: the rows an instance receives land exactly on the rows that it lists as leaving.
All inputs are finite; a program needn't handle non-finite values.
Results may differ from the reference program's by a relative error of at most 0.0034.
Values may be sent and summed in bfloat16 or wider, within the bound.
A program may use at most 64 MiB of HBM per device.

```python
import math
import jax
import jax.numpy as jnp
from jax import lax

ROWS = 32
CTX = 128
HQ = 32
KV = 4
HS = 128
MIG = 4
SLOTS = 256


def migration(key):
    key = jax.random.fold_in(key, 101)
    instances = SLOTS // ROWS
    key_order, key_offset, key_rows = jax.random.split(key, 3)
    shuffle = jax.random.permutation(key_order, instances).astype(jnp.int32)
    inverse = jnp.zeros((instances,), jnp.int32).at[shuffle].set(jnp.arange(instances, dtype=jnp.int32))
    offsets = jax.random.permutation(key_offset, instances - 1)[:MIG].astype(jnp.int32) + 1
    leaving = jax.vmap(lambda single: jax.random.permutation(single, ROWS)[:MIG])(jax.random.split(key_rows, instances)).astype(jnp.int32)
    target = inverse[(shuffle[:, None] + offsets[None, :]) % instances]
    landing = leaving[target, jnp.arange(MIG, dtype=jnp.int32)[None, :]]
    return (leaving, target.astype(jnp.int32), landing.astype(jnp.int32))


def fresh_base(key):
    key = jax.random.fold_in(key, 202)
    key_normal = jax.random.fold_in(key, 0)
    normal = jnp.clip(jax.random.normal(key_normal, (SLOTS, 2, KV * HS), jnp.float32), -4.0, 4.0)
    return normal


def spread(rows_kv):
    row_total = rows_kv.shape[0]
    head_rows = rows_kv.reshape(row_total, KV, 1, HS)
    return jnp.broadcast_to(head_rows, (row_total, KV, HQ // KV, HS)).reshape(row_total, HQ * HS)


def draw_queries(key, part):
    normal = fresh_base(key)
    key = jax.random.fold_in(key, 5)
    jitter = jnp.clip(jax.random.normal(key, (SLOTS, 2, HQ * HS), jnp.float32), -4.0, 4.0)
    earlier_q = 0.35 * spread(normal[:, 0]) + jitter[:, 0]
    second = 0.35 * (spread(normal[:, 0]) + spread(normal[:, 1])) + jitter[:, 1]
    return jnp.stack([earlier_q, second], axis=1).astype(jnp.bfloat16)


def draw_fresh_keys(key, part):
    normal = fresh_base(key)
    return normal.astype(jnp.bfloat16)


def draw_cache_keys(key, part):
    key = jax.random.fold_in(key, 4)
    return jnp.clip(jax.random.normal(key, (SLOTS, CTX, KV * HS), jnp.float32), -4.0, 4.0).astype(jnp.bfloat16)


def draw_cache_values(key, part):
    key = jax.random.fold_in(key, 6)
    key_scale, key_value = jax.random.split(key)
    scales = jnp.exp(jax.random.uniform(key_scale, (SLOTS, CTX, 1), jnp.float32, math.log(0.3), math.log(3.0)))
    return (jnp.clip(jax.random.normal(key_value, (SLOTS, CTX, KV * HS), jnp.float32), -4.0, 4.0) * scales).astype(jnp.bfloat16)


def draw_lengths(key, part):
    key = jax.random.fold_in(key, 7)
    key_cap, key_len, key_pick = jax.random.split(key, 3)
    instances = SLOTS // ROWS
    ceilings = jax.random.randint(key_cap, (instances, 1), 3 * CTX // 4 + 1, CTX - 1)
    row_lengths = jax.random.randint(key_len, (instances, ROWS), ceilings // 2, ceilings + 1).reshape(SLOTS)
    chosen = jax.random.randint(key_pick, (), 0, SLOTS)
    row_lengths = jnp.where(jnp.arange(SLOTS) == chosen, CTX - 2, row_lengths)
    row_lengths = jnp.where(jnp.arange(SLOTS) == (chosen + 1) % SLOTS, 1, row_lengths)
    return row_lengths.astype(jnp.int32)


def draw_move_rows(key, part):
    leaving, target, landing = migration(key)
    return leaving


def draw_move_targets(key, part):
    leaving, target, landing = migration(key)
    return target


def draw_move_landing(key, part):
    leaving, target, landing = migration(key)
    return landing


def shard_levels(own_key, shape, pieces, smallest, high):
    def one(dim, shards_of):
        steps = jax.random.uniform(jax.random.fold_in(jax.random.fold_in(own_key, 6), dim), (shards_of,), jnp.float32, smallest / len(pieces), high / len(pieces))
        return jnp.repeat(jnp.exp(steps), shape[dim] // shards_of).reshape((-1,) + (1,) * (len(shape) - dim - 1))

    loudness = one(*pieces[0])
    for cut in pieces[1:]:
        loudness = loudness * one(*cut)
    return loudness


def noise(stream_key, extent, scale, bound, pieces=(), held_as=jnp.bfloat16):
    array = scale * jax.random.normal(stream_key, extent, jnp.float32)
    if pieces:
        array = array * shard_levels(stream_key, extent, pieces, -0.22, 0.18)
    return jnp.clip(array, -bound, bound).astype(held_as)


def setup_inputs(seed: int = 0, part: int = 0) -> dict:
    streams_of = jax.random.split(jax.random.key(seed), 10)
    own_keys = jax.random.split(jax.random.fold_in(streams_of[9], part), 10)
    return {
        "queries": draw_queries(jax.random.fold_in(jax.random.fold_in(streams_of[9], part), 71), part),
        "fresh_keys": draw_fresh_keys(jax.random.fold_in(jax.random.fold_in(streams_of[9], part), 71), part),
        "fresh_values": noise(own_keys[2], (SLOTS, 2, KV * HS), 1.0, 4.0, ((0, 8), (2, 2))),
        "cache_keys": draw_cache_keys(jax.random.fold_in(jax.random.fold_in(streams_of[9], part), 71), part),
        "cache_values": draw_cache_values(jax.random.fold_in(jax.random.fold_in(streams_of[9], part), 71), part),
        "lengths": draw_lengths(jax.random.fold_in(jax.random.fold_in(streams_of[9], part), 71), part),
        "move_rows": draw_move_rows(jax.random.fold_in(jax.random.fold_in(streams_of[9], part), 71), part),
        "move_targets": draw_move_targets(jax.random.fold_in(jax.random.fold_in(streams_of[9], part), 71), part),
        "move_landing": draw_move_landing(jax.random.fold_in(jax.random.fold_in(streams_of[9], part), 71), part),
    }


masked_score = -1.0e30


def attend_row(query_row, key_rows, value_rows, valid_mask, extra_keys, extra_values):
    group_size = HQ // KV
    shaped = query_row.astype(jnp.float32).reshape(KV, group_size, HS)
    every_key = jnp.concatenate([key_rows, extra_keys], axis=0).astype(jnp.float32).reshape(-1, KV, HS)
    every_value = jnp.concatenate([value_rows, extra_values], axis=0).astype(jnp.float32).reshape(-1, KV, HS)
    usable = jnp.concatenate([valid_mask, jnp.ones((extra_keys.shape[0],), jnp.bool_)])
    scores = jnp.einsum("kgd,pkd->kgp", shaped, every_key) * (HS ** -0.5)
    scores = jnp.where(usable, scores, masked_score)
    maxima = jnp.max(scores, axis=-1, keepdims=True)
    weights = jnp.where(usable, jnp.exp(scores - maxima), 0.0)
    totals = jnp.sum(weights, axis=-1)
    rounded = lax.optimization_barrier(weights.astype(jnp.bfloat16)).astype(jnp.float32)
    mixed = jnp.einsum("kgp,pkd->kgd", rounded, every_value)
    return (mixed / totals[..., None]).reshape(HQ * HS).astype(jnp.bfloat16)


def reference(queries, fresh_keys, fresh_values, cache_keys, cache_values, lengths, move_rows, move_targets, move_landing):
    instances = SLOTS // ROWS
    start_rows = (jnp.arange(instances, dtype=jnp.int32)[:, None] * ROWS + move_rows).reshape(-1).astype(jnp.int32)
    end_rows = (move_targets * ROWS + move_landing).reshape(-1).astype(jnp.int32)
    forward = jnp.arange(SLOTS, dtype=jnp.int32).at[start_rows].set(end_rows)
    anchor = jnp.zeros((SLOTS,), jnp.int32).at[forward].set(jnp.arange(SLOTS, dtype=jnp.int32))
    position = jnp.arange(CTX, dtype=jnp.int32)

    def first_step(row_index):
        valid_mask = position < lengths[row_index]
        return attend_row(queries[row_index, 0], cache_keys[row_index], cache_values[row_index], valid_mask, fresh_keys[row_index, :1], fresh_values[row_index, :1])

    def second_step(slot_index):
        row_index = anchor[slot_index]
        length_now = lengths[row_index]
        valid_mask = position < length_now
        mixed = attend_row(queries[row_index, 1], cache_keys[row_index], cache_values[row_index], valid_mask, fresh_keys[row_index], fresh_values[row_index])
        first_spot = (position == length_now)[:, None]
        second_spot = (position == length_now + 1)[:, None]

        def placed(cached_rows, fresh_rows):
            inside = jnp.where(valid_mask[:, None], cached_rows, jnp.zeros_like(cached_rows))
            return jnp.where(first_spot, fresh_rows[0][None, :], jnp.where(second_spot, fresh_rows[1][None, :], inside))

        return mixed, placed(cache_keys[row_index], fresh_keys[row_index]), placed(cache_values[row_index], fresh_values[row_index])

    first_mixed = lax.map(first_step, jnp.arange(SLOTS, dtype=jnp.int32))
    second_mixed, next_keys, next_values = lax.map(second_step, jnp.arange(SLOTS, dtype=jnp.int32))
    return first_mixed, second_mixed, next_keys, next_values
```

```python
import functools

import jax
import jax.numpy as jnp
from jax import lax
from jax.experimental import pallas as pl
from jax.experimental.pallas import tpu as pltpu
from jax.sharding import PartitionSpec as P

HS = 128
MASKED = -1e30
MESH = pl.DeviceIdType.MESH
UNROLL = 4


def written(cached, fresh, size, place):
    fresh = fresh.astype(jnp.float32)
    cached = cached.astype(jnp.float32)
    out = jnp.where(place < size, cached, 0.0)
    out = jnp.where(place == size, fresh[0:1], out)
    out = jnp.where(place == size + 1, fresh[1:2], out)
    return out.astype(jnp.bfloat16)


def exchange_kernel(
    n,
    lens,
    move_rows,
    move_targets,
    table,
    q,
    fk,
    fv,
    ck_hbm,
    cv_hbm,
    nk,
    nv,
    o_out,
    got,
    got_o,
    got_table,
    ck,
    cv,
    o,
    pack,
    pack_o,
    in_sem,
    out_sem,
    send_sem,
    recv_sem,
):
    me = lax.axis_index("inst")
    rows, ctx, width = ck.shape
    heads = width // HS
    qrows = q.shape[1] // heads
    moves = move_rows.shape[1]

    load_k = pltpu.make_async_copy(ck_hbm, ck, in_sem.at[0])
    load_v = pltpu.make_async_copy(cv_hbm, cv, in_sem.at[1])
    load_k.start()
    load_v.start()

    barrier = pltpu.get_barrier_semaphore()
    for d in range(1, n):
        pl.semaphore_signal(
            barrier, inc=1, device_id={"inst": lax.rem(me + d, n)}, device_id_type=MESH
        )

    place = lax.broadcasted_iota(jnp.int32, (ctx, width), 0)

    def leaving(peer):
        row = jnp.int32(0)
        for j in range(moves):
            row = row + jnp.where(move_targets[0, j] == peer, move_rows[0, j], 0)
        return row

    def remote(src, dst, part, d):
        return pltpu.make_async_remote_copy(
            src_ref=src,
            dst_ref=dst,
            send_sem=send_sem.at[part, d - 1],
            recv_sem=recv_sem.at[part, d - 1],
            device_id={"inst": lax.rem(me + d, n)},
            device_id_type=MESH,
        )

    def send_k(d):
        return remote(pack.at[d - 1, 0], got.at[d - 1, 0], 0, d)

    def send_v(d):
        return remote(pack.at[d - 1, 1], got.at[d - 1, 1], 1, d)

    def send_o(d):
        return remote(pack_o.at[d - 1], got_o.at[d - 1], 2, d)

    def send_table(d):
        return remote(table, got_table.at[d - 1], 3, d)

    load_k.wait()
    pl.semaphore_wait(barrier, n - 1)

    @pl.loop(1, n)
    def _(d):
        row = leaving(lax.rem(me + d, n))
        pack[d - 1, 0] = written(ck[row], fk[row], lens[row], place)
        send_k(d).start()

    load_v.wait()

    @pl.loop(1, n)
    def _(d):
        row = leaving(lax.rem(me + d, n))
        pack[d - 1, 1] = written(cv[row], fv[row], lens[row], place)
        send_v(d).start()

    @pl.loop(1, n)
    def _(d):
        send_table(d).start()

    column = lax.broadcasted_iota(jnp.int32, (qrows, ctx), 1)
    step = jnp.where(lax.broadcasted_iota(jnp.int32, (qrows, ctx), 0) >= qrows // 2, 1, 0)
    offset = column - step
    scale = HS ** (-0.5)

    def save_k(first):
        return pltpu.make_async_copy(
            ck.at[pl.ds(first, UNROLL)], nk.at[pl.ds(first, UNROLL)], out_sem.at[0]
        )

    def save_v(first):
        return pltpu.make_async_copy(
            cv.at[pl.ds(first, UNROLL)], nv.at[pl.ds(first, UNROLL)], out_sem.at[1]
        )

    @pl.loop(0, rows // UNROLL)
    def _(block):
        first = block * UNROLL
        values = []
        scores = []
        for u in range(UNROLL):
            r = first + u
            size = lens[r]
            keys = written(ck[r], fk[r], size, place)
            vals = written(cv[r], fv[r], size, place)
            ck[r] = keys
            cv[r] = vals
            values.append(vals)
            for h in range(heads):
                s = lax.dot_general(
                    q[r, h * qrows : (h + 1) * qrows, :],
                    keys[:, h * HS : (h + 1) * HS],
                    (((1,), (1,)), ((), ())),
                    preferred_element_type=jnp.float32,
                )
                scores.append(jnp.where(offset <= size, s * scale, MASKED))
        save_k(first).start()
        save_v(first).start()
        s = jnp.concatenate(scores, axis=0)
        w = jnp.exp(s - jnp.max(s, axis=1, keepdims=True))
        totals = jnp.sum(w, axis=1, keepdims=True)
        w = w.astype(jnp.bfloat16)
        mixed = []
        for u in range(UNROLL):
            for h in range(heads):
                at = (u * heads + h) * qrows
                mixed.append(
                    lax.dot_general(
                        w[at : at + qrows],
                        values[u][:, h * HS : (h + 1) * HS],
                        (((1,), (0,)), ((), ())),
                        preferred_element_type=jnp.float32,
                    )
                )
        done = (jnp.concatenate(mixed, axis=0) / totals).astype(jnp.bfloat16)
        o[pl.ds(first, UNROLL)] = done.reshape(UNROLL, heads * qrows, HS)

    save_o = pltpu.make_async_copy(o, o_out, in_sem.at[0])
    save_o.start()

    @pl.loop(1, n)
    def _(d):
        row = leaving(lax.rem(me + d, n))
        pack_o[d - 1] = o[row]
        send_o(d).start()

    save_o.wait()
    pltpu.make_async_copy(ck, nk, out_sem.at[0]).wait()
    pltpu.make_async_copy(cv, nv, out_sem.at[1]).wait()

    @pl.loop(1, n)
    def _(d):
        send_table(d).wait()
        send_k(d).wait()
        send_v(d).wait()
        send_o(d).wait()


def place_kernel(
    n, moves, me_ref, table, nk, nv, o, got, got_o, out_k, out_v, out_o, source, sems
):
    rows = nk.shape[0]
    me = me_ref[0]

    @pl.loop(0, rows)
    def _(s):
        source[s] = -1

    @pl.loop(0, n - 1)
    def _(d):
        for j in range(moves):

            @pl.when(table[d, 0, j] == me)
            def _():
                source[table[d, 0, moves + j]] = d

    @pl.loop(0, rows)
    def _(s):
        d = source[s]

        @pl.when(d < 0)
        def _():
            pltpu.make_async_copy(nk.at[s], out_k.at[s], sems.at[0]).start()
            pltpu.make_async_copy(nv.at[s], out_v.at[s], sems.at[1]).start()
            pltpu.make_async_copy(o.at[s], out_o.at[s], sems.at[2]).start()

        @pl.when(d >= 0)
        def _():
            pltpu.make_async_copy(got.at[d, 0], out_k.at[s], sems.at[0]).start()
            pltpu.make_async_copy(got.at[d, 1], out_v.at[s], sems.at[1]).start()
            pltpu.make_async_copy(got_o.at[d], out_o.at[s], sems.at[2]).start()

    pltpu.make_async_copy(nk, out_k, sems.at[0]).wait()
    pltpu.make_async_copy(nv, out_v, sems.at[1]).wait()
    pltpu.make_async_copy(o, out_o, sems.at[2]).wait()


def on_device(
    n,
    queries,
    fresh_keys,
    fresh_values,
    cache_keys,
    cache_values,
    lengths,
    move_rows,
    move_targets,
    move_landing,
):
    rows, ctx, width = cache_keys.shape
    heads = width // HS
    group = queries.shape[2] // HS // heads
    moves = move_rows.shape[1]
    lanes = max(HS, 2 * moves)
    q = (
        queries.reshape(rows, 2, heads, group, HS)
        .transpose(0, 2, 1, 3, 4)
        .reshape(rows, heads * 2 * group, HS)
    )
    table = jnp.pad(
        jnp.concatenate([move_targets, move_landing], axis=1), ((0, 0), (0, lanes - 2 * moves))
    )
    qrows = heads * 2 * group
    bf16 = jnp.bfloat16
    vmem = pl.BlockSpec(memory_space=pltpu.VMEM)
    smem = pl.BlockSpec(memory_space=pltpu.SMEM)
    any_ = pl.BlockSpec(memory_space=pl.ANY)
    shape = jax.ShapeDtypeStruct
    cache = shape((rows, ctx, width), bf16)
    nk, nv, o, got, got_o, got_table = pl.pallas_call(
        functools.partial(exchange_kernel, n),
        out_shape=(
            cache,
            cache,
            shape((rows, qrows, HS), bf16),
            shape((n - 1, 2, ctx, width), bf16),
            shape((n - 1, qrows, HS), bf16),
            shape((n - 1, 1, lanes), jnp.int32),
        ),
        in_specs=[smem, smem, smem, vmem, vmem, vmem, vmem, any_, any_],
        out_specs=(any_,) * 6,
        scratch_shapes=[
            pltpu.VMEM((rows, ctx, width), bf16),
            pltpu.VMEM((rows, ctx, width), bf16),
            pltpu.VMEM((rows, qrows, HS), bf16),
            pltpu.VMEM((n - 1, 2, ctx, width), bf16),
            pltpu.VMEM((n - 1, qrows, HS), bf16),
            pltpu.SemaphoreType.DMA((2,)),
            pltpu.SemaphoreType.DMA((2,)),
            pltpu.SemaphoreType.DMA((4, n - 1)),
            pltpu.SemaphoreType.DMA((4, n - 1)),
        ],
        compiler_params=pltpu.CompilerParams(
            collective_id=0, has_side_effects=True, vmem_limit_bytes=40 * 2**20
        ),
        name="exchange",
    )(lengths, move_rows, move_targets, table, q, fresh_keys, fresh_values, cache_keys, cache_values)
    me = lax.axis_index("inst").astype(jnp.int32).reshape(1)
    next_keys, next_values, settled = pl.pallas_call(
        functools.partial(place_kernel, n, moves),
        out_shape=(cache, cache, shape((rows, qrows, HS), bf16)),
        in_specs=[smem, smem] + [any_] * 5,
        out_specs=(any_,) * 3,
        scratch_shapes=[pltpu.SMEM((rows,), jnp.int32), pltpu.SemaphoreType.DMA((3,))],
        name="place",
    )(me, got_table, nk, nv, o, got, got_o)
    shaped = (rows, heads, 2, group, HS)
    first_mixed = o.reshape(shaped)[:, :, 0].reshape(rows, -1)
    second_mixed = settled.reshape(shaped)[:, :, 1].reshape(rows, -1)
    return first_mixed, second_mixed, next_keys, next_values


def solution(mesh):
    split = P(("groups", "inst"), None, "tp")
    table = P(("groups", "inst"), None)
    return jax.shard_map(
        functools.partial(on_device, mesh.shape["inst"]),
        mesh=mesh,
        in_specs=(split,) * 5 + (P(("groups", "inst")), table, table, table),
        out_specs=(P(("groups", "inst"), "tp"), P(("groups", "inst"), "tp"), split, split),
        check_vma=False,
    )
```

```python
import functools

import jax
import jax.numpy as jnp
from jax import lax
from jax.experimental import pallas as pl
from jax.experimental.pallas import tpu as pltpu
from jax.sharding import PartitionSpec as P

HS = 128
MASKED = -1e30
MESH = pl.DeviceIdType.MESH
TILE = 8
UNROLL = 4


def written(cached, fresh, size, place):
    fresh = fresh.astype(jnp.float32)
    cached = cached.astype(jnp.float32)
    out = jnp.where(place < size, cached, 0.0)
    out = jnp.where(place == size, fresh[0:1], out)
    out = jnp.where(place == size + 1, fresh[1:2], out)
    return out.astype(jnp.bfloat16)


def exchange_kernel(
    n,
    lens_hbm,
    move_rows_hbm,
    move_targets_hbm,
    move_landing_hbm,
    q_hbm,
    fk_hbm,
    fv_hbm,
    ck_hbm,
    cv_hbm,
    nk,
    nv,
    first_out,
    second_out,
    got,
    got_o,
    got_targets,
    got_landing,
    lens,
    move_rows,
    move_targets,
    q,
    fk,
    fv,
    ck,
    cv,
    first_o,
    second_o,
    second_rows,
    pack,
    pack_o,
    in_sem,
    out_sem,
    send_sem,
    recv_sem,
):
    me = lax.axis_index("inst")
    rows, ctx, width = ck.shape
    heads = width // HS
    group = q.shape[2] // width
    moves = move_rows.shape[1]

    loads = [
        pltpu.make_async_copy(src, dst, in_sem.at[i])
        for i, (src, dst) in enumerate(
            (
                (lens_hbm, lens),
                (move_rows_hbm, move_rows),
                (move_targets_hbm, move_targets),
                (fk_hbm, fk),
                (fv_hbm, fv),
                (ck_hbm, ck),
                (cv_hbm, cv),
                (q_hbm, q),
            )
        )
    ]
    for load in loads:
        load.start()

    barrier = pltpu.get_barrier_semaphore()
    for d in range(1, n):
        pl.semaphore_signal(
            barrier, inc=1, device_id={"inst": lax.rem(me + d, n)}, device_id_type=MESH
        )

    place = lax.broadcasted_iota(jnp.int32, (ctx, width), 0)

    def leaving(peer):
        row = jnp.int32(0)
        for j in range(moves):
            row = row + jnp.where(move_targets[0, j] == peer, move_rows[0, j], 0)
        return row

    def remote(src, dst, part, d):
        return pltpu.make_async_remote_copy(
            src_ref=src,
            dst_ref=dst,
            send_sem=send_sem.at[part, d - 1],
            recv_sem=recv_sem.at[part, d - 1],
            device_id={"inst": lax.rem(me + d, n)},
            device_id_type=MESH,
        )

    def send_k(d):
        return remote(pack.at[d - 1, 0], got.at[d - 1, 0], 0, d)

    def send_v(d):
        return remote(pack.at[d - 1, 1], got.at[d - 1, 1], 1, d)

    def send_o(d):
        return remote(pack_o.at[d - 1], got_o.at[d - 1], 2, d)

    def send_targets(d):
        return remote(move_targets_hbm, got_targets.at[d - 1], 3, d)

    def send_landing(d):
        return remote(move_landing_hbm, got_landing.at[d - 1], 4, d)

    for load in loads[:6]:
        load.wait()
    pl.semaphore_wait(barrier, n - 1)

    @pl.loop(1, n)
    def _(d):
        row = leaving(lax.rem(me + d, n))
        pack[d - 1, 0] = written(ck[row], fk[row], lens[row], place)
        send_k(d).start()

    loads[6].wait()

    @pl.loop(1, n)
    def _(d):
        row = leaving(lax.rem(me + d, n))
        pack[d - 1, 1] = written(cv[row], fv[row], lens[row], place)
        send_v(d).start()

    @pl.loop(1, n)
    def _(d):
        send_targets(d).start()
        send_landing(d).start()

    loads[7].wait()
    qrows = 2 * group
    offset = lax.broadcasted_iota(jnp.int32, (qrows, ctx), 1) - lax.rem(
        lax.broadcasted_iota(jnp.int32, (qrows, ctx), 0), 2
    )
    scale = HS ** (-0.5)

    def save_k(first):
        return pltpu.make_async_copy(
            ck.at[pl.ds(first, UNROLL)], nk.at[pl.ds(first, UNROLL)], out_sem.at[0]
        )

    def save_v(first):
        return pltpu.make_async_copy(
            cv.at[pl.ds(first, UNROLL)], nv.at[pl.ds(first, UNROLL)], out_sem.at[1]
        )

    def work(block, low):
        first = block * TILE + low
        values = []
        scores = []
        for u in range(UNROLL):
            r = first + u
            size = lens[r]
            keys = written(ck[r], fk[r], size, place)
            vals = written(cv[r], fv[r], size, place)
            ck[r] = keys
            cv[r] = vals
            values.append(vals)
            query = q[r].astype(jnp.float32)
            for h in range(heads):
                at = h * group
                rows_of = jnp.concatenate(
                    [query[:, (at + g) * HS : (at + g + 1) * HS] for g in range(group)], axis=0
                )
                s = lax.dot_general(
                    rows_of.astype(jnp.bfloat16),
                    keys[:, h * HS : (h + 1) * HS],
                    (((1,), (1,)), ((), ())),
                    preferred_element_type=jnp.float32,
                )
                scores.append(jnp.where(offset <= size, s * scale, MASKED))
        save_k(first).start()
        save_v(first).start()
        s = jnp.concatenate(scores, axis=0)
        w = jnp.exp(s - jnp.max(s, axis=1, keepdims=True))
        totals = jnp.sum(w, axis=1, keepdims=True)
        w = w.astype(jnp.bfloat16)
        for u in range(UNROLL):
            for h in range(heads):
                at = (u * heads + h) * qrows
                mixed = lax.dot_general(
                    w[at : at + qrows],
                    values[u][:, h * HS : (h + 1) * HS],
                    (((1,), (0,)), ((), ())),
                    preferred_element_type=jnp.float32,
                )
                mixed = mixed / totals[at : at + qrows]
                for g in range(group):
                    lanes = pl.ds((h * group + g) * HS, HS)
                    second = mixed[2 * g + 1 : 2 * g + 2]
                    first_o[block, low + u : low + u + 1, lanes] = mixed[2 * g : 2 * g + 1]
                    second_o[block, low + u : low + u + 1, lanes] = second
                    second_rows[first + u, :, lanes] = second

    @pl.loop(0, rows // TILE)
    def _(block):
        for first in range(0, TILE, UNROLL):
            work(block, first)

    saves = [
        pltpu.make_async_copy(first_o, first_out, out_sem.at[2]),
        pltpu.make_async_copy(second_o, second_out, out_sem.at[3]),
    ]
    for save in saves:
        save.start()

    @pl.loop(1, n)
    def _(d):
        row = leaving(lax.rem(me + d, n))
        pack_o[d - 1] = second_rows[row]
        send_o(d).start()

    for save in saves:
        save.wait()
    pltpu.make_async_copy(ck, nk, out_sem.at[0]).wait()
    pltpu.make_async_copy(cv, nv, out_sem.at[1]).wait()

    @pl.loop(1, n)
    def _(d):
        send_targets(d).wait()
        send_landing(d).wait()
        send_k(d).wait()
        send_v(d).wait()
        send_o(d).wait()


def place_kernel(
    n,
    targets_hbm,
    landing_hbm,
    move_rows_hbm,
    nk,
    nv,
    first_hbm,
    second_hbm,
    got,
    got_o,
    out_first,
    out_second,
    out_k,
    out_v,
    targets,
    landing,
    move_rows,
    moved,
    dest,
    k,
    v,
    first,
    second,
    land,
    land_o,
    first_b,
    second_b,
    in_sem,
    chunk_sem,
    land_sem,
    out_sem,
):
    rows = nk.shape[0]
    moves = move_rows.shape[1]
    me = lax.axis_index("inst")
    chunks = chunk_sem.shape[1]
    size = rows // chunks
    small = [
        pltpu.make_async_copy(src, dst, in_sem.at[i])
        for i, (src, dst) in enumerate(
            (
                (move_rows_hbm, move_rows),
                (targets_hbm, targets),
                (landing_hbm, landing),
                (first_hbm, first),
                (second_hbm, second),
            )
        )
    ]
    for copy in small[:3]:
        copy.start()

    def load(c):
        part = pl.ds(c * size, size)
        return (
            pltpu.make_async_copy(nk.at[part], k.at[part], chunk_sem.at[0, c]),
            pltpu.make_async_copy(nv.at[part], v.at[part], chunk_sem.at[1, c]),
        )

    for c in range(chunks):
        for copy in load(c):
            copy.start()
    for copy in small[3:]:
        copy.start()

    @pl.loop(0, rows)
    def _(s):
        moved[s] = 0

    for copy in small[:3]:
        copy.wait()
    for j in range(moves):
        moved[move_rows[0, j]] = 1

    def arrive(d, count):
        row = jnp.int32(0)
        found = jnp.int32(0)
        for j in range(moves):
            mine = targets[d, 0, j] == me
            row = row + jnp.where(mine, landing[d, 0, j], 0)
            found = found + jnp.where(mine, 1, 0)

        @pl.when(found > 0)
        def _():
            dest[count] = row
            pltpu.make_async_copy(got.at[d], land.at[count], land_sem.at[0]).start()
            pltpu.make_async_copy(got_o.at[d], land_o.at[count], land_sem.at[1]).start()

        return count + found

    lax.fori_loop(0, n - 1, arrive, jnp.int32(0))

    for c in range(chunks):
        for copy in load(c):
            copy.wait()

        @pl.loop(c * size, (c + 1) * size)
        def _(s):
            @pl.when(moved[s] == 0)
            def _():
                pltpu.make_async_copy(k.at[s], out_k.at[s], out_sem.at[0]).start()
                pltpu.make_async_copy(v.at[s], out_v.at[s], out_sem.at[1]).start()

    pltpu.make_async_copy(got.at[pl.ds(0, moves)], land, land_sem.at[0]).wait()
    for j in range(moves):
        pltpu.make_async_copy(land.at[j, 0], out_k.at[dest[j]], out_sem.at[0]).start()
        pltpu.make_async_copy(land.at[j, 1], out_v.at[dest[j]], out_sem.at[1]).start()
    for copy in small[3:]:
        copy.wait()
    first_b[...] = first[...].astype(jnp.bfloat16)
    save_first = pltpu.make_async_copy(first_b, out_first, out_sem.at[2])
    save_first.start()
    pltpu.make_async_copy(got_o.at[pl.ds(0, moves)], land_o, land_sem.at[1]).wait()
    settled = second[...]
    slot = lax.broadcasted_iota(jnp.int32, settled.shape, 0)
    for j in range(moves):
        settled = jnp.where(slot == dest[j], land_o[j], settled)
    second_b[...] = settled.astype(jnp.bfloat16)
    save_second = pltpu.make_async_copy(second_b, out_second, out_sem.at[3])
    save_second.start()
    save_first.wait()
    save_second.wait()
    pltpu.make_async_copy(k, out_k, out_sem.at[0]).wait()
    pltpu.make_async_copy(v, out_v, out_sem.at[1]).wait()


def on_device(
    n,
    queries,
    fresh_keys,
    fresh_values,
    cache_keys,
    cache_values,
    lengths,
    move_rows,
    move_targets,
    move_landing,
):
    rows, ctx, width = cache_keys.shape
    wide = queries.shape[2]
    moves = move_rows.shape[1]
    chunks = 4
    tiled = (rows // TILE, TILE, wide)
    bf16, f32, i32 = jnp.bfloat16, jnp.float32, jnp.int32
    hbm = pl.BlockSpec(memory_space=pltpu.HBM)
    shape = jax.ShapeDtypeStruct
    cache = shape((rows, ctx, width), bf16)
    nk, nv, first, second, got, got_o, targets, landing = pl.pallas_call(
        functools.partial(exchange_kernel, n),
        out_shape=(
            cache,
            cache,
            shape(tiled, f32),
            shape(tiled, f32),
            shape((n - 1, 2, ctx, width), bf16),
            shape((n - 1, 1, wide), f32),
            shape((n - 1, 1, moves), i32),
            shape((n - 1, 1, moves), i32),
        ),
        in_specs=[hbm] * 9,
        out_specs=(hbm,) * 8,
        scratch_shapes=[
            pltpu.SMEM((rows,), i32),
            pltpu.SMEM((1, moves), i32),
            pltpu.SMEM((1, moves), i32),
            pltpu.VMEM(queries.shape, bf16),
            pltpu.VMEM(fresh_keys.shape, bf16),
            pltpu.VMEM(fresh_keys.shape, bf16),
            pltpu.VMEM((rows, ctx, width), bf16),
            pltpu.VMEM((rows, ctx, width), bf16),
            pltpu.VMEM(tiled, f32),
            pltpu.VMEM(tiled, f32),
            pltpu.VMEM((rows, 1, wide), f32),
            pltpu.VMEM((n - 1, 2, ctx, width), bf16),
            pltpu.VMEM((n - 1, 1, wide), f32),
            pltpu.SemaphoreType.DMA((8,)),
            pltpu.SemaphoreType.DMA((4,)),
            pltpu.SemaphoreType.DMA((5, n - 1)),
            pltpu.SemaphoreType.DMA((5, n - 1)),
        ],
        compiler_params=pltpu.CompilerParams(
            collective_id=0, has_side_effects=True, vmem_limit_bytes=48 * 2**20
        ),
        name="exchange",
    )(
        lengths,
        move_rows,
        move_targets,
        move_landing,
        queries,
        fresh_keys,
        fresh_values,
        cache_keys,
        cache_values,
    )
    return pl.pallas_call(
        functools.partial(place_kernel, n),
        out_shape=(shape((rows, wide), bf16), shape((rows, wide), bf16), cache, cache),
        in_specs=[hbm] * 9,
        out_specs=(hbm,) * 4,
        scratch_shapes=[
            pltpu.SMEM((n - 1, 1, moves), i32),
            pltpu.SMEM((n - 1, 1, moves), i32),
            pltpu.SMEM((1, moves), i32),
            pltpu.SMEM((rows,), i32),
            pltpu.SMEM((rows,), i32),
            pltpu.VMEM((rows, ctx, width), bf16),
            pltpu.VMEM((rows, ctx, width), bf16),
            pltpu.VMEM((rows, wide), f32),
            pltpu.VMEM((rows, wide), f32),
            pltpu.VMEM((moves, 2, ctx, width), bf16),
            pltpu.VMEM((moves, 1, wide), f32),
            pltpu.VMEM((rows, wide), bf16),
            pltpu.VMEM((rows, wide), bf16),
            pltpu.SemaphoreType.DMA((5,)),
            pltpu.SemaphoreType.DMA((2, chunks)),
            pltpu.SemaphoreType.DMA((2,)),
            pltpu.SemaphoreType.DMA((4,)),
        ],
        compiler_params=pltpu.CompilerParams(vmem_limit_bytes=48 * 2**20),
        name="place",
    )(
        targets,
        landing,
        move_rows,
        nk,
        nv,
        first.reshape(rows, wide),
        second.reshape(rows, wide),
        got,
        got_o,
    )


def solution(mesh):
    split = P(("groups", "inst"), None, "tp")
    table = P(("groups", "inst"), None)
    return jax.shard_map(
        functools.partial(on_device, mesh.shape["inst"]),
        mesh=mesh,
        in_specs=(split,) * 5 + (P(("groups", "inst")), table, table, table),
        out_specs=(P(("groups", "inst"), "tp"), P(("groups", "inst"), "tp"), split, split),
        check_vma=False,
    )
```

```python
import functools

import jax
import jax.numpy as jnp
from jax import lax
from jax.experimental import pallas as pl
from jax.experimental.pallas import tpu as pltpu
from jax.sharding import PartitionSpec as P

HS = 128
MASKED = -1e30
MESH = pl.DeviceIdType.MESH
TILE = 8
UNROLL = 4


def written(cached, fresh, size, place):
    fresh = fresh.astype(jnp.float32)
    cached = cached.astype(jnp.float32)
    out = jnp.where(place < size, cached, 0.0)
    out = jnp.where(place == size, fresh[0:1], out)
    out = jnp.where(place == size + 1, fresh[1:2], out)
    return out.astype(jnp.bfloat16)


def exchange_kernel(
    n,
    lens_hbm,
    move_rows_hbm,
    move_targets_hbm,
    move_landing_hbm,
    q_hbm,
    fk_hbm,
    fv_hbm,
    ck_hbm,
    cv_hbm,
    nk,
    nv,
    first_o,
    second_o,
    got,
    got_o,
    got_targets,
    got_landing,
    lens,
    move_rows,
    move_targets,
    q,
    fk,
    fv,
    ck,
    cv,
    second_rows,
    pack,
    pack_o,
    in_sem,
    send_sem,
    recv_sem,
):
    me = lax.axis_index("inst")
    rows, ctx, width = ck.shape
    heads = width // HS
    group = q.shape[2] // width
    moves = move_rows.shape[1]

    loads = [
        pltpu.make_async_copy(src, dst, in_sem.at[i])
        for i, (src, dst) in enumerate(
            (
                (lens_hbm, lens),
                (move_rows_hbm, move_rows),
                (move_targets_hbm, move_targets),
                (fk_hbm, fk),
                (fv_hbm, fv),
                (ck_hbm, ck),
                (cv_hbm, cv),
                (q_hbm, q),
            )
        )
    ]
    for load in loads[:6]:
        load.start()

    barrier = pltpu.get_barrier_semaphore()
    for d in range(1, n):
        pl.semaphore_signal(
            barrier, inc=1, device_id={"inst": lax.rem(me + d, n)}, device_id_type=MESH
        )

    place = lax.broadcasted_iota(jnp.int32, (ctx, width), 0)

    def leaving(peer):
        row = jnp.int32(0)
        for j in range(moves):
            row = row + jnp.where(move_targets[0, j] == peer, move_rows[0, j], 0)
        return row

    def remote(src, dst, part, d):
        return pltpu.make_async_remote_copy(
            src_ref=src,
            dst_ref=dst,
            send_sem=send_sem.at[part, d - 1],
            recv_sem=recv_sem.at[part, d - 1],
            device_id={"inst": lax.rem(me + d, n)},
            device_id_type=MESH,
        )

    def send_k(d):
        return remote(pack.at[d - 1, 0], got.at[d - 1, 0], 0, d)

    def send_v(d):
        return remote(pack.at[d - 1, 1], got.at[d - 1, 1], 1, d)

    def send_o(d):
        return remote(pack_o.at[d - 1], got_o.at[d - 1], 2, d)

    def send_targets(d):
        return remote(move_targets_hbm, got_targets.at[d - 1], 3, d)

    def send_landing(d):
        return remote(move_landing_hbm, got_landing.at[d - 1], 4, d)

    for load in loads[:6]:
        load.wait()
    for load in loads[6:]:
        load.start()
    pl.semaphore_wait(barrier, n - 1)

    @pl.loop(1, n)
    def _(d):
        row = leaving(lax.rem(me + d, n))
        pack[d - 1, 0] = written(ck[row], fk[row], lens[row], place)
        send_k(d).start()

    loads[6].wait()

    @pl.loop(1, n)
    def _(d):
        row = leaving(lax.rem(me + d, n))
        pack[d - 1, 1] = written(cv[row], fv[row], lens[row], place)
        send_v(d).start()

    @pl.loop(1, n)
    def _(d):
        send_targets(d).start()
        send_landing(d).start()

    loads[7].wait()
    qrows = 2 * group
    offset = lax.broadcasted_iota(jnp.int32, (qrows, ctx), 1) - lax.rem(
        lax.broadcasted_iota(jnp.int32, (qrows, ctx), 0), 2
    )
    scale = HS ** (-0.5)

    def work(block, low):
        first = block * TILE + low
        values = []
        scores = []
        for u in range(UNROLL):
            r = first + u
            size = lens[r]
            keys = written(ck[r], fk[r], size, place)
            vals = written(cv[r], fv[r], size, place)
            nk[r] = keys
            nv[r] = vals
            values.append(vals)
            query = q[r].astype(jnp.float32)
            for h in range(heads):
                at = h * group
                rows_of = jnp.concatenate(
                    [query[:, (at + g) * HS : (at + g + 1) * HS] for g in range(group)], axis=0
                )
                s = lax.dot_general(
                    rows_of.astype(jnp.bfloat16),
                    keys[:, h * HS : (h + 1) * HS],
                    (((1,), (1,)), ((), ())),
                    preferred_element_type=jnp.float32,
                )
                scores.append(jnp.where(offset <= size, s * scale, MASKED))
        s = jnp.concatenate(scores, axis=0)
        w = jnp.exp(s - jnp.max(s, axis=1, keepdims=True))
        totals = jnp.sum(w, axis=1, keepdims=True)
        w = w.astype(jnp.bfloat16)
        for u in range(UNROLL):
            for h in range(heads):
                at = (u * heads + h) * qrows
                mixed = lax.dot_general(
                    w[at : at + qrows],
                    values[u][:, h * HS : (h + 1) * HS],
                    (((1,), (0,)), ((), ())),
                    preferred_element_type=jnp.float32,
                )
                mixed = mixed / totals[at : at + qrows]
                for g in range(group):
                    lanes = pl.ds((h * group + g) * HS, HS)
                    second = mixed[2 * g + 1 : 2 * g + 2]
                    first_o[block, low + u : low + u + 1, lanes] = mixed[2 * g : 2 * g + 1]
                    second_o[block, low + u : low + u + 1, lanes] = second
                    second_rows[first + u, :, lanes] = second

    @pl.loop(0, rows // TILE)
    def _(block):
        for first in range(0, TILE, UNROLL):
            work(block, first)

    @pl.loop(1, n)
    def _(d):
        row = leaving(lax.rem(me + d, n))
        pack_o[d - 1] = second_rows[row]
        send_o(d).start()

    @pl.loop(1, n)
    def _(d):
        send_targets(d).wait()
        send_landing(d).wait()
        send_k(d).wait()
        send_v(d).wait()
        send_o(d).wait()


def place_kernel(
    n,
    targets_hbm,
    landing_hbm,
    move_rows_hbm,
    nk,
    nv,
    first,
    second,
    got,
    got_o,
    out_first,
    out_second,
    out_k,
    out_v,
    targets,
    landing,
    move_rows,
    moved,
    dest,
    origin,
    first_b,
    second_b,
    in_sem,
    out_sem,
):
    rows = nk.shape[0]
    moves = move_rows.shape[1]
    me = lax.axis_index("inst")
    small = [
        pltpu.make_async_copy(src, dst, in_sem.at[i])
        for i, (src, dst) in enumerate(
            (
                (move_rows_hbm, move_rows),
                (targets_hbm, targets),
                (landing_hbm, landing),
            )
        )
    ]
    for copy in small:
        copy.start()

    first_b[...] = first[...].astype(jnp.bfloat16)
    save_first = pltpu.make_async_copy(first_b, out_first, out_sem.at[2])
    save_first.start()

    @pl.loop(0, rows)
    def _(s):
        moved[s] = 0

    for copy in small:
        copy.wait()
    for j in range(moves):
        moved[move_rows[0, j]] = 1

    @pl.loop(0, rows)
    def _(s):
        @pl.when(moved[s] == 0)
        def _():
            pltpu.make_async_copy(nk.at[s], out_k.at[s], out_sem.at[0]).start()
            pltpu.make_async_copy(nv.at[s], out_v.at[s], out_sem.at[1]).start()

    def arrive(d, count):
        row = jnp.int32(0)
        found = jnp.int32(0)
        for j in range(moves):
            mine = targets[d, 0, j] == me
            row = row + jnp.where(mine, landing[d, 0, j], 0)
            found = found + jnp.where(mine, 1, 0)

        @pl.when(found > 0)
        def _():
            dest[count] = row
            origin[count] = d
            pltpu.make_async_copy(got.at[d, 0], out_k.at[row], out_sem.at[0]).start()
            pltpu.make_async_copy(got.at[d, 1], out_v.at[row], out_sem.at[1]).start()

        return count + found

    lax.fori_loop(0, n - 1, arrive, jnp.int32(0))
    settled = second[...]
    slot = lax.broadcasted_iota(jnp.int32, settled.shape, 0)
    for j in range(moves):
        settled = jnp.where(slot == dest[j], got_o[origin[j]], settled)
    second_b[...] = settled.astype(jnp.bfloat16)
    save_second = pltpu.make_async_copy(second_b, out_second, out_sem.at[3])
    save_second.start()
    save_first.wait()
    save_second.wait()
    pltpu.make_async_copy(nk, out_k, out_sem.at[0]).wait()
    pltpu.make_async_copy(nv, out_v, out_sem.at[1]).wait()


def on_device(
    n,
    queries,
    fresh_keys,
    fresh_values,
    cache_keys,
    cache_values,
    lengths,
    move_rows,
    move_targets,
    move_landing,
):
    rows, ctx, width = cache_keys.shape
    wide = queries.shape[2]
    moves = move_rows.shape[1]
    tiled = (rows // TILE, TILE, wide)
    bf16, f32, i32 = jnp.bfloat16, jnp.float32, jnp.int32
    hbm = pl.BlockSpec(memory_space=pltpu.HBM)
    vmem = pl.BlockSpec(memory_space=pltpu.VMEM)
    shape = jax.ShapeDtypeStruct
    cache = shape((rows, ctx, width), bf16)
    nk, nv, first, second, got, got_o, targets, landing = pl.pallas_call(
        functools.partial(exchange_kernel, n),
        out_shape=(
            pltpu.VMEM((rows, ctx, width), bf16),
            pltpu.VMEM((rows, ctx, width), bf16),
            pltpu.VMEM(tiled, f32),
            pltpu.VMEM(tiled, f32),
            pltpu.VMEM((n - 1, 2, ctx, width), bf16),
            pltpu.VMEM((n - 1, 1, wide), f32),
            pltpu.VMEM((n - 1, 1, moves), i32),
            pltpu.VMEM((n - 1, 1, moves), i32),
        ),
        in_specs=[hbm] * 9,
        out_specs=(vmem,) * 8,
        scratch_shapes=[
            pltpu.SMEM((rows,), i32),
            pltpu.SMEM((1, moves), i32),
            pltpu.SMEM((1, moves), i32),
            pltpu.VMEM(queries.shape, bf16),
            pltpu.VMEM(fresh_keys.shape, bf16),
            pltpu.VMEM(fresh_keys.shape, bf16),
            pltpu.VMEM((rows, ctx, width), bf16),
            pltpu.VMEM((rows, ctx, width), bf16),
            pltpu.VMEM((rows, 1, wide), f32),
            pltpu.VMEM((n - 1, 2, ctx, width), bf16),
            pltpu.VMEM((n - 1, 1, wide), f32),
            pltpu.SemaphoreType.DMA((8,)),
            pltpu.SemaphoreType.DMA((5, n - 1)),
            pltpu.SemaphoreType.DMA((5, n - 1)),
        ],
        compiler_params=pltpu.CompilerParams(
            collective_id=0, has_side_effects=True, vmem_limit_bytes=32 * 2**20
        ),
        name="exchange",
    )(
        *(
            pltpu.with_memory_space_constraint(x, pltpu.HBM)
            for x in (
                lengths,
                move_rows,
                move_targets,
                move_landing,
                queries,
                fresh_keys,
                fresh_values,
                cache_keys,
                cache_values,
            )
        )
    )
    return pl.pallas_call(
        functools.partial(place_kernel, n),
        out_shape=(shape((rows, wide), bf16), shape((rows, wide), bf16), cache, cache),
        in_specs=[vmem, vmem, hbm] + [vmem] * 6,
        out_specs=(hbm,) * 4,
        scratch_shapes=[
            pltpu.SMEM((n - 1, 1, moves), i32),
            pltpu.SMEM((n - 1, 1, moves), i32),
            pltpu.SMEM((1, moves), i32),
            pltpu.SMEM((rows,), i32),
            pltpu.SMEM((rows,), i32),
            pltpu.SMEM((rows,), i32),
            pltpu.VMEM((rows, wide), bf16),
            pltpu.VMEM((rows, wide), bf16),
            pltpu.SemaphoreType.DMA((3,)),
            pltpu.SemaphoreType.DMA((4,)),
        ],
        compiler_params=pltpu.CompilerParams(vmem_limit_bytes=32 * 2**20),
        name="place",
    )(
        targets,
        landing,
        move_rows,
        nk,
        nv,
        first.reshape(rows, wide),
        second.reshape(rows, wide),
        got,
        got_o,
    )


def solution(mesh):
    split = P(("groups", "inst"), None, "tp")
    table = P(("groups", "inst"), None)
    return jax.shard_map(
        functools.partial(on_device, mesh.shape["inst"]),
        mesh=mesh,
        in_specs=(split,) * 5 + (P(("groups", "inst")), table, table, table),
        out_specs=(P(("groups", "inst"), "tp"), P(("groups", "inst"), "tp"), split, split),
        check_vma=False,
    )
```

```python
import functools

import jax
import jax.numpy as jnp
from jax import lax
from jax.experimental import pallas as pl
from jax.experimental.pallas import tpu as pltpu
from jax.sharding import PartitionSpec as P

HS = 128
MASKED = -1e30
MESH = pl.DeviceIdType.MESH
TILE = 8
UNROLL = 4


def written(cached, fresh, size, place):
    fresh = fresh.astype(jnp.float32)
    cached = cached.astype(jnp.float32)
    out = jnp.where(place < size, cached, 0.0)
    out = jnp.where(place == size, fresh[0:1], out)
    out = jnp.where(place == size + 1, fresh[1:2], out)
    return out.astype(jnp.bfloat16)


def exchange_kernel(
    n,
    lens_hbm,
    move_rows_hbm,
    move_targets_hbm,
    move_landing_hbm,
    q_hbm,
    fk_hbm,
    fv_hbm,
    ck_hbm,
    cv_hbm,
    nk,
    nv,
    first_o,
    second_o,
    got,
    got_o,
    got_targets,
    got_landing,
    lens,
    move_rows,
    move_targets,
    q,
    fk,
    fv,
    ck,
    cv,
    second_rows,
    pack,
    pack_o,
    in_sem,
    send_sem,
    recv_sem,
):
    me = lax.axis_index("inst")
    rows, ctx, width = ck.shape
    heads = width // HS
    group = q.shape[2] // width
    moves = move_rows.shape[1]

    loads = [
        pltpu.make_async_copy(src, dst, in_sem.at[i])
        for i, (src, dst) in enumerate(
            (
                (lens_hbm, lens),
                (move_rows_hbm, move_rows),
                (move_targets_hbm, move_targets),
                (fk_hbm, fk),
                (fv_hbm, fv),
                (ck_hbm, ck),
                (cv_hbm, cv),
                (q_hbm, q),
            )
        )
    ]
    for load in loads[:6]:
        load.start()

    barrier = pltpu.get_barrier_semaphore()
    for d in range(1, n):
        pl.semaphore_signal(
            barrier, inc=1, device_id={"inst": lax.rem(me + d, n)}, device_id_type=MESH
        )

    place = lax.broadcasted_iota(jnp.int32, (ctx, width), 0)

    def leaving(peer):
        row = jnp.int32(0)
        for j in range(moves):
            row = row + jnp.where(move_targets[0, j] == peer, move_rows[0, j], 0)
        return row

    def remote(src, dst, part, d):
        return pltpu.make_async_remote_copy(
            src_ref=src,
            dst_ref=dst,
            send_sem=send_sem.at[part, d - 1],
            recv_sem=recv_sem.at[part, d - 1],
            device_id={"inst": lax.rem(me + d, n)},
            device_id_type=MESH,
        )

    def send_k(d):
        return remote(pack.at[d - 1, 0], got.at[d - 1, 0], 0, d)

    def send_v(d):
        return remote(pack.at[d - 1, 1], got.at[d - 1, 1], 1, d)

    def send_o(d):
        return remote(pack_o.at[d - 1], got_o.at[d - 1], 2, d)

    def send_targets(d):
        return remote(move_targets_hbm, got_targets.at[d - 1], 3, d)

    def send_landing(d):
        return remote(move_landing_hbm, got_landing.at[d - 1], 4, d)

    for load in loads[:6]:
        load.wait()
    for load in loads[6:]:
        load.start()
    pl.semaphore_wait(barrier, n - 1)

    @pl.loop(1, n)
    def _(d):
        row = leaving(lax.rem(me + d, n))
        pack[d - 1, 0] = written(ck[row], fk[row], lens[row], place)
        send_k(d).start()

    loads[6].wait()

    @pl.loop(1, n)
    def _(d):
        row = leaving(lax.rem(me + d, n))
        pack[d - 1, 1] = written(cv[row], fv[row], lens[row], place)
        send_v(d).start()

    @pl.loop(1, n)
    def _(d):
        send_targets(d).start()
        send_landing(d).start()

    loads[7].wait()
    qrows = 2 * group
    offset = (
        lax.broadcasted_iota(jnp.int32, (qrows, ctx), 1)
        - lax.broadcasted_iota(jnp.int32, (qrows, ctx), 0) // group
    )
    scale = HS ** (-0.5)

    def work(block, low):
        first = block * TILE + low
        values = []
        scores = []
        for u in range(UNROLL):
            r = first + u
            size = lens[r]
            keys = written(ck[r], fk[r], size, place)
            vals = written(cv[r], fv[r], size, place)
            nk[r] = keys
            nv[r] = vals
            values.append(vals)
            query = q[r].astype(jnp.float32)
            for h in range(heads):
                at = h * group
                rows_of = jnp.concatenate(
                    [
                        query[t : t + 1, (at + g) * HS : (at + g + 1) * HS]
                        for t in range(2)
                        for g in range(group)
                    ],
                    axis=0,
                )
                s = lax.dot_general(
                    rows_of.astype(jnp.bfloat16),
                    keys[:, h * HS : (h + 1) * HS],
                    (((1,), (1,)), ((), ())),
                    preferred_element_type=jnp.float32,
                )
                scores.append(jnp.where(offset <= size, s * scale, MASKED))
        s = jnp.concatenate(scores, axis=0)
        w = jnp.exp(s - jnp.max(s, axis=1, keepdims=True))
        totals = jnp.sum(w, axis=1, keepdims=True)
        w = w.astype(jnp.bfloat16)
        for u in range(UNROLL):
            seconds = []
            for h in range(heads):
                at = (u * heads + h) * qrows
                mixed = lax.dot_general(
                    w[at : at + qrows],
                    values[u][:, h * HS : (h + 1) * HS],
                    (((1,), (0,)), ((), ())),
                    preferred_element_type=jnp.float32,
                )
                mixed = mixed / totals[at : at + qrows]
                for g in range(group):
                    lanes = pl.ds((h * group + g) * HS, HS)
                    second = mixed[group + g : group + g + 1]
                    first_o[block, low + u : low + u + 1, lanes] = mixed[g : g + 1]
                    second_o[block, low + u : low + u + 1, lanes] = second
                seconds.append(mixed[group:])
            second_rows[first + u] = jnp.concatenate(seconds, axis=0).astype(jnp.bfloat16)

    @pl.loop(0, rows // TILE)
    def _(block):
        for first in range(0, TILE, UNROLL):
            work(block, first)

    @pl.loop(1, n)
    def _(d):
        row = leaving(lax.rem(me + d, n))
        pack_o[d - 1] = second_rows[row]
        send_o(d).start()

    @pl.loop(1, n)
    def _(d):
        send_targets(d).wait()
        send_landing(d).wait()
        send_k(d).wait()
        send_v(d).wait()
        send_o(d).wait()


def place_kernel(
    n,
    targets_hbm,
    landing_hbm,
    move_rows_hbm,
    nk,
    nv,
    first,
    second,
    got,
    got_o,
    out_first,
    out_second,
    out_k,
    out_v,
    targets,
    landing,
    move_rows,
    moved,
    dest,
    origin,
    first_b,
    second_b,
    in_sem,
    out_sem,
):
    rows = nk.shape[0]
    moves = move_rows.shape[1]
    me = lax.axis_index("inst")
    small = [
        pltpu.make_async_copy(src, dst, in_sem.at[i])
        for i, (src, dst) in enumerate(
            (
                (move_rows_hbm, move_rows),
                (targets_hbm, targets),
                (landing_hbm, landing),
            )
        )
    ]
    for copy in small:
        copy.start()

    first_b[...] = first[...].astype(jnp.bfloat16)
    save_first = pltpu.make_async_copy(first_b, out_first, out_sem.at[2])
    save_first.start()

    @pl.loop(0, rows)
    def _(s):
        moved[s] = 0

    for copy in small:
        copy.wait()
    for j in range(moves):
        moved[move_rows[0, j]] = 1

    @pl.loop(0, rows)
    def _(s):
        @pl.when(moved[s] == 0)
        def _():
            pltpu.make_async_copy(nk.at[s], out_k.at[s], out_sem.at[0]).start()
            pltpu.make_async_copy(nv.at[s], out_v.at[s], out_sem.at[1]).start()

    def arrive(d, count):
        row = jnp.int32(0)
        found = jnp.int32(0)
        for j in range(moves):
            mine = targets[d, 0, j] == me
            row = row + jnp.where(mine, landing[d, 0, j], 0)
            found = found + jnp.where(mine, 1, 0)

        @pl.when(found > 0)
        def _():
            dest[count] = row
            origin[count] = d
            pltpu.make_async_copy(got.at[d, 0], out_k.at[row], out_sem.at[0]).start()
            pltpu.make_async_copy(got.at[d, 1], out_v.at[row], out_sem.at[1]).start()

        return count + found

    lax.fori_loop(0, n - 1, arrive, jnp.int32(0))
    slot = lax.broadcasted_iota(jnp.int32, (rows, HS), 0)
    incoming = [got_o[origin[j]].astype(jnp.float32) for j in range(moves)]
    for i in range(got_o.shape[1]):
        lanes = slice(i * HS, (i + 1) * HS)
        part = second[:, lanes]
        for j in range(moves):
            part = jnp.where(slot == dest[j], incoming[j][i : i + 1], part)
        second_b[:, lanes] = part.astype(jnp.bfloat16)
    save_second = pltpu.make_async_copy(second_b, out_second, out_sem.at[3])
    save_second.start()
    save_first.wait()
    save_second.wait()
    pltpu.make_async_copy(nk, out_k, out_sem.at[0]).wait()
    pltpu.make_async_copy(nv, out_v, out_sem.at[1]).wait()


def on_device(
    n,
    queries,
    fresh_keys,
    fresh_values,
    cache_keys,
    cache_values,
    lengths,
    move_rows,
    move_targets,
    move_landing,
):
    rows, ctx, width = cache_keys.shape
    wide = queries.shape[2]
    moves = move_rows.shape[1]
    tiled = (rows // TILE, TILE, wide)
    bf16, f32, i32 = jnp.bfloat16, jnp.float32, jnp.int32
    hbm = pl.BlockSpec(memory_space=pltpu.HBM)
    vmem = pl.BlockSpec(memory_space=pltpu.VMEM)
    shape = jax.ShapeDtypeStruct
    cache = shape((rows, ctx, width), bf16)
    nk, nv, first, second, got, got_o, targets, landing = pl.pallas_call(
        functools.partial(exchange_kernel, n),
        out_shape=(
            pltpu.VMEM((rows, ctx, width), bf16),
            pltpu.VMEM((rows, ctx, width), bf16),
            pltpu.VMEM(tiled, f32),
            pltpu.VMEM(tiled, f32),
            pltpu.VMEM((n - 1, 2, ctx, width), bf16),
            pltpu.VMEM((n - 1, wide // HS, HS), bf16),
            pltpu.VMEM((n - 1, 1, moves), i32),
            pltpu.VMEM((n - 1, 1, moves), i32),
        ),
        in_specs=[hbm] * 9,
        out_specs=(vmem,) * 8,
        scratch_shapes=[
            pltpu.SMEM((rows,), i32),
            pltpu.SMEM((1, moves), i32),
            pltpu.SMEM((1, moves), i32),
            pltpu.VMEM(queries.shape, bf16),
            pltpu.VMEM(fresh_keys.shape, bf16),
            pltpu.VMEM(fresh_keys.shape, bf16),
            pltpu.VMEM((rows, ctx, width), bf16),
            pltpu.VMEM((rows, ctx, width), bf16),
            pltpu.VMEM((rows, wide // HS, HS), bf16),
            pltpu.VMEM((n - 1, 2, ctx, width), bf16),
            pltpu.VMEM((n - 1, wide // HS, HS), bf16),
            pltpu.SemaphoreType.DMA((8,)),
            pltpu.SemaphoreType.DMA((5, n - 1)),
            pltpu.SemaphoreType.DMA((5, n - 1)),
        ],
        compiler_params=pltpu.CompilerParams(
            collective_id=0, has_side_effects=True, vmem_limit_bytes=32 * 2**20
        ),
        name="exchange",
    )(
        *(
            pltpu.with_memory_space_constraint(x, pltpu.HBM)
            for x in (
                lengths,
                move_rows,
                move_targets,
                move_landing,
                queries,
                fresh_keys,
                fresh_values,
                cache_keys,
                cache_values,
            )
        )
    )
    return pl.pallas_call(
        functools.partial(place_kernel, n),
        out_shape=(shape((rows, wide), bf16), shape((rows, wide), bf16), cache, cache),
        in_specs=[vmem, vmem, hbm] + [vmem] * 6,
        out_specs=(hbm,) * 4,
        scratch_shapes=[
            pltpu.SMEM((n - 1, 1, moves), i32),
            pltpu.SMEM((n - 1, 1, moves), i32),
            pltpu.SMEM((1, moves), i32),
            pltpu.SMEM((rows,), i32),
            pltpu.SMEM((rows,), i32),
            pltpu.SMEM((rows,), i32),
            pltpu.VMEM((rows, wide), bf16),
            pltpu.VMEM((rows, wide), bf16),
            pltpu.SemaphoreType.DMA((3,)),
            pltpu.SemaphoreType.DMA((4,)),
        ],
        compiler_params=pltpu.CompilerParams(vmem_limit_bytes=32 * 2**20),
        name="place",
    )(
        targets,
        landing,
        move_rows,
        nk,
        nv,
        first.reshape(rows, wide),
        second.reshape(rows, wide),
        got,
        got_o,
    )


def solution(mesh):
    split = P(("groups", "inst"), None, "tp")
    table = P(("groups", "inst"), None)
    return jax.shard_map(
        functools.partial(on_device, mesh.shape["inst"]),
        mesh=mesh,
        in_specs=(split,) * 5 + (P(("groups", "inst")), table, table, table),
        out_specs=(P(("groups", "inst"), "tp"), P(("groups", "inst"), "tp"), split, split),
        check_vma=False,
    )
```
